32 devices in a mesh: groups: 2 (over y), ctx: 4 (over x, core), head: 4 (over z).
Axes of the slice: x: 2, y: 2, z: 4, core: 2. Of those that a mesh axis runs over, the one named last changes fastest.
Arguments:
- queries: bfloat16 [12288, 512], P(('groups', 'ctx', 'head')), parts along dimension 0, may hold values from -8 to 8
- keys: bfloat16 [12288, 512], P(('groups', 'ctx', 'head')), parts along dimension 0, may hold values from -8 to 8
- values: bfloat16 [12288, 512], P(('groups', 'ctx', 'head')), parts along dimension 0, may hold values from -6 to 6
- tile_lists: int32 [96, 16], P(('groups', 'ctx')), parts along dimension 0, may hold values from -8 to 54, as said below
- live_counts: int32 [96], P(('groups', 'ctx')), parts along dimension 0, may hold values from 8 to 16
Outputs:
- attended: bfloat16 [12288, 512], P(('groups', 'ctx', 'head')), parts along dimension 0
The draws below stay inside these ranges and needn't reach their ends.
There are 2 independent parts, one for each index of `groups`. The reference program is written for one: setup_inputs(seed, part) draws one part's arguments, and reference() takes and returns one part's arrays. A program takes and returns all parts, laid end to end along the dimension named above; each array names one. Nothing has to cross between parts.
Inputs may be any that keep to these rules, and one draw needn't show every extreme that they name: `tile_lists`: row t holds t + o for each offset o from -8 to 7 exactly once, the first entry being t itself; entries outside 0 to 47 occur only near the ends of the video.
All inputs are finite; a program needn't handle non-finite values.
Results may differ from the reference program's by a relative error of at most 0.0047.
Values may be sent and summed in bfloat16 or wider, within the bound.
A program may use at most 64 MiB of HBM per device.

```python
import jax
import jax.numpy as jnp
from jax import lax

HDIM = 128
TILE = 128
EDGE = 8
LIST = 16
HEADS = 4
NTILES = 48
TOKENS = 6144


def draw_queries(key, part):
    sample = jax.random.normal(jax.random.fold_in(key, 1), (TOKENS, HEADS * HDIM), jnp.float32)
    sample = jnp.clip(sample, -8.0, 8.0)
    return sample.astype(jnp.bfloat16)


def draw_keys(key, part):
    sample = jax.random.normal(jax.random.fold_in(key, 2), (TOKENS, HEADS * HDIM), jnp.float32)
    sample = jnp.clip(sample, -8.0, 8.0)
    return sample.astype(jnp.bfloat16)


def draw_tile_lists(key, part):
    others = jnp.concatenate([jnp.arange(-EDGE, 0), jnp.arange(1, EDGE)]).astype(jnp.int32)
    row_keys = jax.random.split(jax.random.fold_in(key, 3), NTILES)
    shuffled = jax.vmap(lambda row_key: jax.random.permutation(row_key, others))(row_keys)
    offsets = jnp.concatenate([jnp.zeros((NTILES, 1), jnp.int32), shuffled.astype(jnp.int32)], axis=1)
    return (jnp.arange(NTILES, dtype=jnp.int32)[:, None] + offsets).astype(jnp.int32)


def draw_live_counts(key, part):
    counts = jax.random.randint(jax.random.fold_in(key, 4), (NTILES,), LIST // 2, LIST + 1).astype(jnp.int32)
    counts = counts.at[0].set(LIST)
    return counts.at[1].set(LIST // 2)


def steps_of(stream_key, shape, shards, smallest, high):
    level, own = 1.0, jax.random.fold_in(stream_key, 6)
    for axis_at, shards_of in shards:
        steps = jnp.exp(jax.random.uniform(jax.random.fold_in(own, axis_at), (shards_of,), jnp.float32, smallest / len(shards), high / len(shards)))
        level = level * jnp.repeat(steps, shape[axis_at] // shards_of).reshape([-1 if axis == axis_at else 1 for axis in range(len(shape))])
    return level


def normal_values(own_key, dims, spread, limit, cuts=(), held_as=jnp.bfloat16):
    gain = steps_of(own_key, dims, cuts, -0.22, 0.18) if cuts else 1.0
    entries = jax.random.normal(own_key, dims, jnp.float32) * spread * gain
    return jnp.minimum(jnp.maximum(entries, -limit), limit).astype(held_as)


def setup_inputs(seed: int = 0, part: int = 0) -> dict:
    seeds = jax.random.split(jax.random.key(seed), 6)
    own_keys = jax.random.split(jax.random.fold_in(seeds[5], part), 6)
    queries = draw_queries(jax.random.fold_in(jax.random.fold_in(seeds[5], part), 71), part)
    keys = draw_keys(jax.random.fold_in(jax.random.fold_in(seeds[5], part), 71), part)
    values = normal_values(own_keys[2], (TOKENS, HEADS * HDIM), 1.0, 6.0, ((0, 16),))
    tile_lists = draw_tile_lists(jax.random.fold_in(jax.random.fold_in(seeds[5], part), 71), part)
    live_counts = draw_live_counts(jax.random.fold_in(jax.random.fold_in(seeds[5], part), 71), part)
    return dict(queries=queries, keys=keys, values=values, tile_lists=tile_lists, live_counts=live_counts)


def reference(queries, keys, values, tile_lists, live_counts):
    score_scale = HDIM ** -0.5

    def per_heads(array):
        return array.astype(jnp.float32).reshape(NTILES, TILE, HEADS, HDIM).transpose(2, 0, 1, 3)

    positions = jnp.arange(LIST)
    usable = (positions[None, :] < live_counts[:, None]) & (tile_lists >= 0) & (tile_lists < NTILES)
    safe_tiles = jnp.clip(tile_lists, 0, NTILES - 1).astype(jnp.int32)
    visible = jnp.repeat(usable, TILE, axis=1)[:, None, :]

    def per_head(inputs):
        q_head, k_head, v_head = inputs
        k_picked = k_head[safe_tiles].reshape(NTILES, LIST * TILE, HDIM)
        v_picked = v_head[safe_tiles].reshape(NTILES, LIST * TILE, HDIM)
        scores = jnp.einsum("tqd,tkd->tqk", q_head, k_picked, precision=lax.Precision.HIGHEST) * score_scale
        scores = jnp.where(visible, scores, -1e30)
        highest = jnp.max(scores, axis=-1, keepdims=True)
        weights = jnp.where(visible, jnp.exp(scores - highest), 0.0)
        softmax_divisor = jnp.sum(weights, axis=-1, keepdims=True)
        rounded = lax.optimization_barrier(weights.astype(jnp.bfloat16))
        attention_probs = rounded.astype(jnp.float32)
        mixed = jnp.einsum("tqk,tkd->tqd", attention_probs, v_picked, precision=lax.Precision.HIGHEST)
        return (mixed / softmax_divisor).astype(jnp.bfloat16)

    results = lax.map(per_head, (per_heads(queries), per_heads(keys), per_heads(values)))
    return results.transpose(1, 2, 0, 3).reshape(TOKENS, HEADS * HDIM)
```

```python
import functools
import math

import jax
import jax.numpy as jnp
from jax import lax
from jax.experimental import pallas as pl
from jax.experimental.pallas import tpu as pltpu
from jax.sharding import PartitionSpec as P

HDIM = 128
TILE = 128
EDGE = 8
HALO = EDGE * TILE
MASKED = -1e30
MESH = pl.DeviceIdType.MESH
K, V, Q = 0, 1, 2


def partner(me, d, n):
    if n & (n - 1):
        return lax.rem(me + d, n)
    out, bit = 0, 1
    while bit < n:
        mine = lax.rem(me // bit, 2)
        flip = (d // bit) % 2
        out = out + bit * (mine + flip * (1 - 2 * mine))
        bit *= 2
    return out


def kernel(
    n, ctx_count, tiles, group,
    counts_ref, lists_ref, q_ref, k_ref, v_ref, out_ref,
    qa, ka, va, oscr, bias,
    send_sem, recv_sem, halo_send, halo_recv, o_send, o_recv, own_sem,
):
    rows = q_ref.shape[0]
    total = tiles * TILE
    me = lax.axis_index("head")
    c = lax.axis_index("ctx")
    order = sorted(range(1, n), reverse=True)

    barrier = pltpu.get_barrier_semaphore()
    for d in range(1, n):
        pl.semaphore_signal(barrier, 1, device_id={"head": partner(me, d, n)}, device_id_type=MESH)

    @pl.when(c > 0)
    def _():
        pl.semaphore_signal(barrier, 1, device_id={"ctx": c - 1}, device_id_type=MESH)

    @pl.when(c < ctx_count - 1)
    def _():
        pl.semaphore_signal(barrier, 1, device_id={"ctx": c + 1}, device_id_type=MESH)

    def columns(s):
        return pl.ds(pl.multiple_of(s * HDIM, HDIM), HDIM)

    sources = (k_ref, v_ref, q_ref)
    targets = (ka, va, qa)
    firsts = (HALO, HALO, 0)

    def landing(kind, s):
        first = firsts[kind] + s * rows
        return targets[kind].at[pl.ds(pl.multiple_of(first, 16), rows), pl.ds(0, HDIM)]

    def own(kind):
        return pltpu.make_async_copy(
            sources[kind].at[:, columns(me)], landing(kind, me), recv_sem.at[kind, me]
        )

    def send(kind, d):
        s = partner(me, d, n)
        return pltpu.make_async_remote_copy(
            src_ref=sources[kind].at[:, columns(s)],
            dst_ref=landing(kind, me),
            send_sem=send_sem.at[kind, d],
            recv_sem=recv_sem.at[kind, me],
            device_id={"head": s},
            device_id_type=MESH,
        )

    def arrived(kind, s):
        there = landing(kind, s)
        pltpu.make_async_copy(there, there, recv_sem.at[kind, s]).wait()

    @pl.when(jnp.logical_and(c > 0, c < ctx_count - 1))
    def _():
        pl.semaphore_wait(barrier, n + 1)

    @pl.when(jnp.logical_or(c == 0, c == ctx_count - 1))
    def _():
        pl.semaphore_wait(barrier, n)

    for kind in (K, V, Q):
        for d in order:
            send(kind, d).start()
        own(kind).start()

    @pl.when(c == 0)
    def _():
        ka[pl.ds(0, HALO), pl.ds(0, HDIM)] = jnp.zeros((HALO, HDIM), jnp.bfloat16)
        va[pl.ds(0, HALO), pl.ds(0, HDIM)] = jnp.zeros((HALO, HDIM), jnp.bfloat16)

    @pl.when(c == ctx_count - 1)
    def _():
        ka[pl.ds(HALO + total, HALO), pl.ds(0, HDIM)] = jnp.zeros((HALO, HDIM), jnp.bfloat16)
        va[pl.ds(HALO + total, HALO), pl.ds(0, HDIM)] = jnp.zeros((HALO, HDIM), jnp.bfloat16)

    window_tiles = tiles + 2 * EDGE
    lanes = lax.broadcasted_iota(jnp.int32, (TILE, HDIM), 1)
    for t in range(window_tiles):
        ka[pl.ds(t * TILE, TILE), pl.ds(HDIM, HDIM)] = jnp.where(lanes == t, 1.0, 0.0).astype(jnp.bfloat16)
    va[:, pl.ds(HDIM, HDIM)] = jnp.ones((window_tiles * TILE, HDIM), jnp.bfloat16)

    row = lax.broadcasted_iota(jnp.int32, (tiles, HDIM), 0)
    ids = lax.broadcasted_iota(jnp.int32, (tiles, HDIM), 1) + (c * tiles - EDGE)
    count = jnp.zeros((tiles, HDIM), jnp.int32)
    for t in range(tiles):
        count = jnp.where(row == t, counts_ref[t], count)
    entries = lists_ref[...]
    hits = jnp.zeros((tiles, HDIM), jnp.int32)
    for j in range(entries.shape[1]):
        hit = jnp.logical_and(entries[:, j : j + 1] == ids, count > j)
        hits = jnp.where(hit, 1, hits)
    inside = jnp.logical_and(ids >= 0, ids < tiles * ctx_count)
    bias[...] = jnp.where(jnp.logical_and(hits > 0, inside), 0.0, MASKED)
    for t in range(tiles):
        mask = jnp.broadcast_to(bias[pl.ds(t, 1), :], (TILE, HDIM))
        qa[pl.ds(t * TILE, TILE), pl.ds(HDIM, HDIM)] = mask.astype(jnp.bfloat16)

    def halo_copies(s):
        out = []
        low, high = max(s * rows, total - HALO), (s + 1) * rows
        if low < high:
            out.append((0, c < ctx_count - 1, c > 0, c + 1, low, low - (total - HALO), high - low))
        low, high = s * rows, min((s + 1) * rows, HALO)
        if low < high:
            out.append((1, c > 0, c < ctx_count - 1, c - 1, low, HALO + total + low, high - low))
        return out

    def halo(kind, s, side, to, low, there, size):
        return pltpu.make_async_remote_copy(
            src_ref=targets[kind].at[pl.ds(HALO + low, size), pl.ds(0, HDIM)],
            dst_ref=targets[kind].at[pl.ds(there, size), pl.ds(0, HDIM)],
            send_sem=halo_send.at[kind, side, s],
            recv_sem=halo_recv.at[kind, side, s],
            device_id={"ctx": to},
            device_id_type=MESH,
        )

    for kind in (K, V):
        for s in range(n):
            arrived(kind, s)
            for side, sends, _, to, low, there, size in halo_copies(s):
                @pl.when(sends)
                def _():
                    halo(kind, s, side, to, low, there, size).start()

    for kind in (K, V):
        for s in range(n):
            for side, _, gets, to, low, there, size in halo_copies(s):
                @pl.when(gets)
                def _():
                    halo(kind, s, side, to, low, there, size).wait_recv()

    factor = HDIM ** (-0.5) * math.log2(math.e)

    def attend(g):
        size = group * TILE
        span = size + 2 * HALO - TILE
        first = pl.multiple_of(g * size, TILE)
        scores = lax.dot_general(
            qa[pl.ds(first, size), :], ka[pl.ds(first, span), :],
            (((1,), (1,)), ((), ())), preferred_element_type=jnp.float32,
        )
        highest = jnp.max(scores, axis=1, keepdims=True)
        weights = jnp.exp2((scores - highest) * factor).astype(jnp.bfloat16)
        mixed = jnp.dot(weights, va[pl.ds(first, span), :], preferred_element_type=jnp.float32)
        oscr[pl.ds(first, size), :] = (mixed[:, :HDIM] / mixed[:, HDIM:]).astype(jnp.bfloat16)

    def o_rows(s):
        return oscr.at[pl.ds(pl.multiple_of(s * rows, 16), rows), :]

    def give(d):
        s = partner(me, d, n)
        return pltpu.make_async_remote_copy(
            src_ref=o_rows(s),
            dst_ref=out_ref.at[:, columns(me)],
            send_sem=o_send.at[d],
            recv_sem=o_recv.at[me],
            device_id={"head": s},
            device_id_type=MESH,
        )

    keep = pltpu.make_async_copy(o_rows(me), out_ref.at[:, columns(me)], own_sem)
    if rows == group * TILE:
        for d in range(n):
            s = partner(me, d, n)
            arrived(Q, s)
            attend(s)
            if d:
                give(d).start()
            else:
                keep.start()
    else:
        for s in range(n):
            arrived(Q, s)

        def step(g, carry):
            attend(g)
            return carry

        lax.fori_loop(0, tiles // group, step, 0)
        for d in range(1, n):
            give(d).start()
        keep.start()

    for kind in (K, V, Q):
        for d in order:
            send(kind, d).wait_send()
    for kind in (K, V):
        for s in range(n):
            for side, sends, _, to, low, there, size in halo_copies(s):
                @pl.when(sends)
                def _():
                    halo(kind, s, side, to, low, there, size).wait_send()
    keep.wait()
    for d in range(1, n):
        s = partner(me, d, n)
        there = out_ref.at[:, columns(s)]
        give(d).wait_send()
        pltpu.make_async_copy(there, there, o_recv.at[s]).wait()


def on_device(n, ctx_count, queries, keys, values, tile_lists, live_counts):
    tiles = tile_lists.shape[0]
    total = tiles * TILE
    window = total + 2 * HALO
    group = 3 if tiles % 3 == 0 else 1
    dma = pltpu.SemaphoreType.DMA
    return pl.pallas_call(
        functools.partial(kernel, n, ctx_count, tiles, group),
        out_shape=jax.ShapeDtypeStruct(queries.shape, jnp.bfloat16),
        in_specs=[
            pl.BlockSpec(memory_space=pltpu.SMEM),
            pl.BlockSpec(memory_space=pltpu.VMEM),
            pl.BlockSpec(memory_space=pl.ANY),
            pl.BlockSpec(memory_space=pl.ANY),
            pl.BlockSpec(memory_space=pl.ANY),
        ],
        out_specs=pl.BlockSpec(memory_space=pl.ANY),
        scratch_shapes=[
            pltpu.VMEM((total, 2 * HDIM), jnp.bfloat16),
            pltpu.VMEM((window, 2 * HDIM), jnp.bfloat16),
            pltpu.VMEM((window, 2 * HDIM), jnp.bfloat16),
            pltpu.VMEM((total, HDIM), jnp.bfloat16),
            pltpu.VMEM((tiles, HDIM), jnp.float32),
            dma((3, n)),
            dma((3, n)),
            dma((2, 2, n)),
            dma((2, 2, n)),
            dma((n,)),
            dma((n,)),
            dma,
        ],
        compiler_params=pltpu.CompilerParams(
            collective_id=0, has_side_effects=True, vmem_limit_bytes=48 << 20
        ),
    )(live_counts, tile_lists, queries, keys, values)


def solution(mesh):
    return jax.shard_map(
        functools.partial(on_device, mesh.shape["head"], mesh.shape["ctx"]),
        mesh=mesh,
        in_specs=(
            P(("groups", "ctx", "head"), None),
            P(("groups", "ctx", "head"), None),
            P(("groups", "ctx", "head"), None),
            P(("groups", "ctx"), None),
            P(("groups", "ctx")),
        ),
        out_specs=P(("groups", "ctx", "head"), None),
        check_vma=False,
    )
```

```python
import functools
import math

import jax
import jax.numpy as jnp
from jax import lax
from jax.experimental import pallas as pl
from jax.experimental.pallas import tpu as pltpu
from jax.sharding import PartitionSpec as P

HDIM = 128
TILE = 128
EDGE = 8
HALO = EDGE * TILE
MASKED = -1e30
MESH = pl.DeviceIdType.MESH
K, V = 0, 1


def partner(me, d, n):
    if n & (n - 1):
        return lax.rem(me + d, n)
    out, bit = 0, 1
    while bit < n:
        mine = lax.rem(me // bit, 2)
        flip = (d // bit) % 2
        out = out + bit * (mine + flip * (1 - 2 * mine))
        bit *= 2
    return out


def kernel(
    n, ctx_count, tiles, group,
    counts_in, lists_in, q_ref, k_ref, v_ref, out_ref,
    counts_ref, lists_ref, qa, ka, va, oscr, bias,
    send_sem, recv_sem, q_sent, q_recv, halo_send, halo_recv, o_send, o_recv, own_sem,
):
    rows = q_ref.shape[0]
    staged = rows == group * TILE and n == 4
    pieces = group if staged else 1
    part = rows // pieces
    total = tiles * TILE
    me = lax.axis_index("head")
    c = lax.axis_index("ctx")
    order = list(range(1, n))

    barrier = pltpu.get_barrier_semaphore()
    for d in range(1, n):
        pl.semaphore_signal(barrier, 1, device_id={"head": partner(me, d, n)}, device_id_type=MESH)

    @pl.when(c > 0)
    def _():
        pl.semaphore_signal(barrier, 1, device_id={"ctx": c - 1}, device_id_type=MESH)

    @pl.when(c < ctx_count - 1)
    def _():
        pl.semaphore_signal(barrier, 1, device_id={"ctx": c + 1}, device_id_type=MESH)

    def columns(s):
        return pl.ds(pl.multiple_of(s * HDIM, HDIM), HDIM)

    sources = (k_ref, v_ref)
    targets = (ka, va)

    def landing(kind, s):
        first = HALO + s * rows
        return targets[kind].at[pl.ds(pl.multiple_of(first, 16), rows), pl.ds(0, HDIM)]

    def own(kind):
        return pltpu.make_async_copy(
            sources[kind].at[:, columns(me)], landing(kind, me), recv_sem.at[kind, me]
        )

    def send(kind, d):
        s = partner(me, d, n)
        return pltpu.make_async_remote_copy(
            src_ref=sources[kind].at[:, columns(s)],
            dst_ref=landing(kind, me),
            send_sem=send_sem.at[kind, d],
            recv_sem=recv_sem.at[kind, me],
            device_id={"head": s},
            device_id_type=MESH,
        )

    def arrived(kind, s):
        there = landing(kind, s)
        pltpu.make_async_copy(there, there, recv_sem.at[kind, s]).wait()

    def q_landing(s, p):
        first = pl.multiple_of(s * rows + p * part, 16)
        return qa.at[pl.ds(first, part), pl.ds(0, HDIM)]

    def q_own(p):
        return pltpu.make_async_copy(
            q_ref.at[pl.ds(p * part, part), columns(me)], q_landing(me, p), q_recv.at[me, p]
        )

    def q_send(d, p):
        s = partner(me, d, n)
        return pltpu.make_async_remote_copy(
            src_ref=q_ref.at[pl.ds(p * part, part), columns(s)],
            dst_ref=q_landing(me, p),
            send_sem=q_sent.at[d, p],
            recv_sem=q_recv.at[me, p],
            device_id={"head": s},
            device_id_type=MESH,
        )

    def q_arrived(s, p):
        there = q_landing(s, p)
        pltpu.make_async_copy(there, there, q_recv.at[s, p]).wait()

    @pl.when(jnp.logical_and(c > 0, c < ctx_count - 1))
    def _():
        pl.semaphore_wait(barrier, n + 1)

    @pl.when(jnp.logical_or(c == 0, c == ctx_count - 1))
    def _():
        pl.semaphore_wait(barrier, n)

    for kind in (K, V):
        for d in order:
            send(kind, d).start()
        own(kind).start()
    for p in range(pieces):
        q_own(p).start()
    if not staged:
        for d in order:
            q_send(d, 0).start()

    counts_copy = pltpu.make_async_copy(counts_in, counts_ref, own_sem.at[1])
    lists_copy = pltpu.make_async_copy(lists_in, lists_ref, own_sem.at[2])
    counts_copy.start()
    lists_copy.start()

    @pl.when(c == 0)
    def _():
        ka[pl.ds(0, HALO), pl.ds(0, HDIM)] = jnp.zeros((HALO, HDIM), jnp.bfloat16)
        va[pl.ds(0, HALO), pl.ds(0, HDIM)] = jnp.zeros((HALO, HDIM), jnp.bfloat16)

    @pl.when(c == ctx_count - 1)
    def _():
        ka[pl.ds(HALO + total, HALO), pl.ds(0, HDIM)] = jnp.zeros((HALO, HDIM), jnp.bfloat16)
        va[pl.ds(HALO + total, HALO), pl.ds(0, HDIM)] = jnp.zeros((HALO, HDIM), jnp.bfloat16)

    window_tiles = tiles + 2 * EDGE
    lanes = lax.broadcasted_iota(jnp.int32, (TILE, HDIM), 1)
    for t in range(window_tiles):
        ka[pl.ds(t * TILE, TILE), pl.ds(HDIM, HDIM)] = jnp.where(lanes == t, 1.0, 0.0).astype(jnp.bfloat16)
    va[:, pl.ds(HDIM, HDIM)] = jnp.ones((window_tiles * TILE, HDIM), jnp.bfloat16)

    counts_copy.wait()
    lists_copy.wait()
    row = lax.broadcasted_iota(jnp.int32, (tiles, HDIM), 0)
    ids = lax.broadcasted_iota(jnp.int32, (tiles, HDIM), 1) + (c * tiles - EDGE)
    count = jnp.zeros((tiles, HDIM), jnp.int32)
    for t in range(tiles):
        count = jnp.where(row == t, counts_ref[t], count)
    entries = lists_ref[...]
    hits = jnp.zeros((tiles, HDIM), jnp.int32)
    for j in range(entries.shape[1]):
        hit = jnp.logical_and(entries[:, j : j + 1] == ids, count > j)
        hits = jnp.where(hit, 1, hits)
    inside = jnp.logical_and(ids >= 0, ids < tiles * ctx_count)
    bias[...] = jnp.where(jnp.logical_and(hits > 0, inside), 0.0, MASKED)
    for t in range(tiles):
        mask = jnp.broadcast_to(bias[pl.ds(t, 1), :], (TILE, HDIM))
        qa[pl.ds(t * TILE, TILE), pl.ds(HDIM, HDIM)] = mask.astype(jnp.bfloat16)

    def halo_copies(s):
        out = []
        low, high = max(s * rows, total - HALO), (s + 1) * rows
        if low < high:
            out.append((0, c < ctx_count - 1, c > 0, c + 1, low, low - (total - HALO), high - low))
        low, high = s * rows, min((s + 1) * rows, HALO)
        if low < high:
            out.append((1, c > 0, c < ctx_count - 1, c - 1, low, HALO + total + low, high - low))
        return out

    def halo(kind, s, side, to, low, there, size):
        return pltpu.make_async_remote_copy(
            src_ref=targets[kind].at[pl.ds(HALO + low, size), pl.ds(0, HDIM)],
            dst_ref=targets[kind].at[pl.ds(there, size), pl.ds(0, HDIM)],
            send_sem=halo_send.at[kind, side, s],
            recv_sem=halo_recv.at[kind, side, s],
            device_id={"ctx": to},
            device_id_type=MESH,
        )

    if staged:
        for kind in (K, V):
            send(kind, 2).wait_send()
            if kind == K:
                q_send(2, 0).start()
                q_send(2, 1).start()
            else:
                q_send(2, 2).start()
                for p in range(pieces):
                    q_send(1, p).start()

    for kind in (K, V):
        for s in range(n):
            arrived(kind, s)
            for side, sends, _, to, low, there, size in halo_copies(s):
                @pl.when(sends)
                def _():
                    halo(kind, s, side, to, low, there, size).start()

    if staged:
        for p in range(pieces):
            q_send(2, p).wait_send()
            q_send(3, p).start()

    for kind in (K, V):
        for s in range(n):
            for side, _, gets, to, low, there, size in halo_copies(s):
                @pl.when(gets)
                def _():
                    halo(kind, s, side, to, low, there, size).wait_recv()

    factor = HDIM ** (-0.5) * math.log2(math.e)

    def attend(first, size):
        span = size + 2 * HALO - TILE
        first = pl.multiple_of(first, TILE)
        scores = lax.dot_general(
            qa[pl.ds(first, size), :], ka[pl.ds(first, span), :],
            (((1,), (1,)), ((), ())), preferred_element_type=jnp.float32,
        )
        highest = jnp.max(scores, axis=1, keepdims=True)
        weights = jnp.exp2((scores - highest) * factor).astype(jnp.bfloat16)
        mixed = jnp.dot(weights, va[pl.ds(first, span), :], preferred_element_type=jnp.float32)
        oscr[pl.ds(first, size), :] = (mixed[:, :HDIM] / mixed[:, HDIM:]).astype(jnp.bfloat16)

    def give(d, p):
        s = partner(me, d, n)
        return pltpu.make_async_remote_copy(
            src_ref=oscr.at[pl.ds(pl.multiple_of(s * rows + p * part, 16), part), :],
            dst_ref=out_ref.at[pl.ds(p * part, part), columns(me)],
            send_sem=o_send.at[d, p],
            recv_sem=o_recv.at[me, p],
            device_id={"head": s},
            device_id_type=MESH,
        )

    keep = pltpu.make_async_copy(
        oscr.at[pl.ds(pl.multiple_of(me * rows, 16), rows), :], out_ref.at[:, columns(me)],
        own_sem.at[0],
    )
    if staged:
        for d in (2, 1, 3):
            s = partner(me, d, n)
            for p in range(pieces):
                q_arrived(s, p)
                attend(s * rows + p * TILE, TILE)
                give(d, p).start()
        for p in range(pieces):
            q_arrived(me, p)
        attend(me * rows, rows)
    else:
        for s in range(n):
            q_arrived(s, 0)

        def step(g, carry):
            attend(g * group * TILE, group * TILE)
            return carry

        lax.fori_loop(0, tiles // group, step, 0)
        for d in range(1, n):
            give(d, 0).start()
    keep.start()

    for kind in (K, V):
        for d in order:
            if not (staged and d == 2):
                send(kind, d).wait_send()
    for d in order:
        for p in range(pieces):
            if not (staged and d == 2):
                q_send(d, p).wait_send()
    for kind in (K, V):
        for s in range(n):
            for side, sends, _, to, low, there, size in halo_copies(s):
                @pl.when(sends)
                def _():
                    halo(kind, s, side, to, low, there, size).wait_send()
    keep.wait()
    for d in range(1, n):
        s = partner(me, d, n)
        for p in range(pieces):
            there = out_ref.at[pl.ds(p * part, part), columns(s)]
            give(d, p).wait_send()
            pltpu.make_async_copy(there, there, o_recv.at[s, p]).wait()


def on_device(n, ctx_count, queries, keys, values, tile_lists, live_counts):
    tiles = tile_lists.shape[0]
    total = tiles * TILE
    window = total + 2 * HALO
    group = 3 if tiles % 3 == 0 else 1
    dma = pltpu.SemaphoreType.DMA
    return pl.pallas_call(
        functools.partial(kernel, n, ctx_count, tiles, group),
        out_shape=jax.ShapeDtypeStruct(queries.shape, jnp.bfloat16),
        in_specs=[
            pl.BlockSpec(memory_space=pltpu.HBM),
            pl.BlockSpec(memory_space=pltpu.HBM),
            pl.BlockSpec(memory_space=pltpu.HBM),
            pl.BlockSpec(memory_space=pltpu.HBM),
            pl.BlockSpec(memory_space=pltpu.HBM),
        ],
        out_specs=pl.BlockSpec(memory_space=pltpu.HBM),
        scratch_shapes=[
            pltpu.SMEM(live_counts.shape, jnp.int32),
            pltpu.VMEM(tile_lists.shape, jnp.int32),
            pltpu.VMEM((total, 2 * HDIM), jnp.bfloat16),
            pltpu.VMEM((window, 2 * HDIM), jnp.bfloat16),
            pltpu.VMEM((window, 2 * HDIM), jnp.bfloat16),
            pltpu.VMEM((total, HDIM), jnp.bfloat16),
            pltpu.VMEM((tiles, HDIM), jnp.float32),
            dma((2, n)),
            dma((2, n)),
            dma((n, group)),
            dma((n, group)),
            dma((2, 2, n)),
            dma((2, 2, n)),
            dma((n, group)),
            dma((n, group)),
            dma((3,)),
        ],
        compiler_params=pltpu.CompilerParams(
            collective_id=0, has_side_effects=True, vmem_limit_bytes=63 << 20
        ),
    )(live_counts, tile_lists, queries, keys, values)


def solution(mesh):
    return jax.shard_map(
        functools.partial(on_device, mesh.shape["head"], mesh.shape["ctx"]),
        mesh=mesh,
        in_specs=(
            P(("groups", "ctx", "head"), None),
            P(("groups", "ctx", "head"), None),
            P(("groups", "ctx", "head"), None),
            P(("groups", "ctx"), None),
            P(("groups", "ctx")),
        ),
        out_specs=P(("groups", "ctx", "head"), None),
        check_vma=False,
    )
```

```python
import functools
import math

import jax
import jax.numpy as jnp
from jax import lax
from jax.experimental import pallas as pl
from jax.experimental.pallas import tpu as pltpu
from jax.sharding import PartitionSpec as P

HDIM = 128
TILE = 128
EDGE = 8
HALO = EDGE * TILE
MASKED = -1e30
MESH = pl.DeviceIdType.MESH
K, V = 0, 1


def partner(me, d, n):
    if n & (n - 1):
        return lax.rem(me + d, n)
    out, bit = 0, 1
    while bit < n:
        mine = lax.rem(me // bit, 2)
        flip = (d // bit) % 2
        out = out + bit * (mine + flip * (1 - 2 * mine))
        bit *= 2
    return out


def kernel(
    n, ctx_count, tiles, group,
    counts_in, lists_in, q_ref, k_ref, v_ref, out_ref,
    counts_ref, lists_ref, qa, ka, va, oscr, bias,
    send_sem, recv_sem, q_sent, q_recv, halo_send, halo_recv, o_send, o_recv, own_sem,
):
    rows = q_ref.shape[0]
    staged = rows == group * TILE and n == 4
    pieces = group if staged else 1
    part = rows // pieces
    total = tiles * TILE
    me = lax.axis_index("head")
    c = lax.axis_index("ctx")
    order = list(range(1, n))

    barrier = pltpu.get_barrier_semaphore()
    for d in range(1, n):
        pl.semaphore_signal(barrier, 1, device_id={"head": partner(me, d, n)}, device_id_type=MESH)

    @pl.when(c > 0)
    def _():
        pl.semaphore_signal(barrier, 1, device_id={"ctx": c - 1}, device_id_type=MESH)

    @pl.when(c < ctx_count - 1)
    def _():
        pl.semaphore_signal(barrier, 1, device_id={"ctx": c + 1}, device_id_type=MESH)

    def columns(s):
        return pl.ds(pl.multiple_of(s * HDIM, HDIM), HDIM)

    sources = (k_ref, v_ref)
    targets = (ka, va)

    def landing(kind, s):
        first = HALO + s * rows
        return targets[kind].at[pl.ds(pl.multiple_of(first, 16), rows), pl.ds(0, HDIM)]

    def own(kind):
        return pltpu.make_async_copy(
            sources[kind].at[:, columns(me)], landing(kind, me), recv_sem.at[kind, me]
        )

    def send(kind, d):
        s = partner(me, d, n)
        return pltpu.make_async_remote_copy(
            src_ref=sources[kind].at[:, columns(s)],
            dst_ref=landing(kind, me),
            send_sem=send_sem.at[kind, d],
            recv_sem=recv_sem.at[kind, me],
            device_id={"head": s},
            device_id_type=MESH,
        )

    def arrived(kind, s):
        there = landing(kind, s)
        pltpu.make_async_copy(there, there, recv_sem.at[kind, s]).wait()

    def q_landing(s, p):
        first = pl.multiple_of(s * rows + p * part, 16)
        return qa.at[pl.ds(first, part), pl.ds(0, HDIM)]

    def q_own(p):
        return pltpu.make_async_copy(
            q_ref.at[pl.ds(p * part, part), columns(me)], q_landing(me, p), q_recv.at[me, p]
        )

    def q_send(d, p):
        s = partner(me, d, n)
        return pltpu.make_async_remote_copy(
            src_ref=q_ref.at[pl.ds(p * part, part), columns(s)],
            dst_ref=q_landing(me, p),
            send_sem=q_sent.at[d, p],
            recv_sem=q_recv.at[me, p],
            device_id={"head": s},
            device_id_type=MESH,
        )

    def q_arrived(s, p):
        there = q_landing(s, p)
        pltpu.make_async_copy(there, there, q_recv.at[s, p]).wait()

    @pl.when(jnp.logical_and(c > 0, c < ctx_count - 1))
    def _():
        pl.semaphore_wait(barrier, n + 1)

    @pl.when(jnp.logical_or(c == 0, c == ctx_count - 1))
    def _():
        pl.semaphore_wait(barrier, n)

    for kind in (K, V):
        for d in order:
            send(kind, d).start()
        own(kind).start()
    for p in range(pieces):
        q_own(p).start()
    if not staged:
        for d in order:
            q_send(d, 0).start()

    counts_copy = pltpu.make_async_copy(counts_in, counts_ref, own_sem.at[1])
    lists_copy = pltpu.make_async_copy(lists_in, lists_ref, own_sem.at[2])
    counts_copy.start()
    lists_copy.start()

    @pl.when(c == 0)
    def _():
        ka[pl.ds(0, HALO), pl.ds(0, HDIM)] = jnp.zeros((HALO, HDIM), jnp.bfloat16)
        va[pl.ds(0, HALO), pl.ds(0, HDIM)] = jnp.zeros((HALO, HDIM), jnp.bfloat16)

    @pl.when(c == ctx_count - 1)
    def _():
        ka[pl.ds(HALO + total, HALO), pl.ds(0, HDIM)] = jnp.zeros((HALO, HDIM), jnp.bfloat16)
        va[pl.ds(HALO + total, HALO), pl.ds(0, HDIM)] = jnp.zeros((HALO, HDIM), jnp.bfloat16)

    window_tiles = tiles + 2 * EDGE
    lanes = lax.broadcasted_iota(jnp.int32, (TILE, HDIM), 1)
    for t in range(window_tiles):
        ka[pl.ds(t * TILE, TILE), pl.ds(HDIM, HDIM)] = jnp.where(lanes == t, 1.0, 0.0).astype(jnp.bfloat16)
    va[:, pl.ds(HDIM, HDIM)] = jnp.ones((window_tiles * TILE, HDIM), jnp.bfloat16)

    counts_copy.wait()
    lists_copy.wait()
    row = lax.broadcasted_iota(jnp.int32, (tiles, HDIM), 0)
    ids = lax.broadcasted_iota(jnp.int32, (tiles, HDIM), 1) + (c * tiles - EDGE)
    count = jnp.zeros((tiles, HDIM), jnp.int32)
    for t in range(tiles):
        count = jnp.where(row == t, counts_ref[t], count)
    entries = lists_ref[...]
    hits = jnp.zeros((tiles, HDIM), jnp.int32)
    for j in range(entries.shape[1]):
        hit = jnp.logical_and(entries[:, j : j + 1] == ids, count > j)
        hits = jnp.where(hit, 1, hits)
    inside = jnp.logical_and(ids >= 0, ids < tiles * ctx_count)
    bias[...] = jnp.where(jnp.logical_and(hits > 0, inside), 0.0, MASKED)
    for t in range(tiles):
        mask = jnp.broadcast_to(bias[pl.ds(t, 1), :], (TILE, HDIM))
        qa[pl.ds(t * TILE, TILE), pl.ds(HDIM, HDIM)] = mask.astype(jnp.bfloat16)

    def halo_copies(s):
        out = []
        low, high = max(s * rows, total - HALO), (s + 1) * rows
        if low < high:
            out.append((0, c < ctx_count - 1, c > 0, c + 1, low, low - (total - HALO), high - low))
        low, high = s * rows, min((s + 1) * rows, HALO)
        if low < high:
            out.append((1, c > 0, c < ctx_count - 1, c - 1, low, HALO + total + low, high - low))
        return out

    def halo(kind, s, side, to, low, there, size):
        return pltpu.make_async_remote_copy(
            src_ref=targets[kind].at[pl.ds(HALO + low, size), pl.ds(0, HDIM)],
            dst_ref=targets[kind].at[pl.ds(there, size), pl.ds(0, HDIM)],
            send_sem=halo_send.at[kind, side, s],
            recv_sem=halo_recv.at[kind, side, s],
            device_id={"ctx": to},
            device_id_type=MESH,
        )

    if staged:
        for kind in (K, V):
            send(kind, 2).wait_send()
            if kind == K:
                q_send(2, 0).start()
                q_send(2, 1).start()
            else:
                q_send(2, 2).start()
                for p in range(pieces):
                    q_send(1, p).start()

    for kind in (K, V):
        for s in range(n):
            arrived(kind, s)
            for side, sends, _, to, low, there, size in halo_copies(s):
                @pl.when(sends)
                def _():
                    halo(kind, s, side, to, low, there, size).start()

    if staged:
        for p in range(pieces):
            q_send(2, p).wait_send()
            q_send(3, p).start()

    for kind in (K, V):
        for s in range(n):
            for side, _, gets, to, low, there, size in halo_copies(s):
                @pl.when(gets)
                def _():
                    halo(kind, s, side, to, low, there, size).wait_recv()

    factor = HDIM ** (-0.5) * math.log2(math.e)

    def attend(first, size):
        span = size + 2 * HALO - TILE
        first = pl.multiple_of(first, TILE)
        scores = lax.dot_general(
            qa[pl.ds(first, size), :], ka[pl.ds(first, span), :],
            (((1,), (1,)), ((), ())), preferred_element_type=jnp.float32,
        )
        highest = jnp.max(scores, axis=1, keepdims=True)
        weights = jnp.exp2((scores - highest) * factor).astype(jnp.bfloat16)
        mixed = jnp.dot(weights, va[pl.ds(first, span), :], preferred_element_type=jnp.float32)
        oscr[pl.ds(first, size), :] = (mixed[:, :HDIM] / mixed[:, HDIM:]).astype(jnp.bfloat16)

    def give(d, p):
        s = partner(me, d, n)
        return pltpu.make_async_remote_copy(
            src_ref=oscr.at[pl.ds(pl.multiple_of(s * rows + p * part, 16), part), :],
            dst_ref=out_ref.at[pl.ds(p * part, part), columns(me)],
            send_sem=o_send.at[d, p],
            recv_sem=o_recv.at[me, p],
            device_id={"head": s},
            device_id_type=MESH,
        )

    keep = pltpu.make_async_copy(
        oscr.at[pl.ds(pl.multiple_of(me * rows, 16), rows), :], out_ref.at[:, columns(me)],
        own_sem.at[0],
    )
    if staged:
        for d in (2, 1, 3, 0):
            s = partner(me, d, n)
            if d in (0, 1, 2):
                for p in range(pieces):
                    q_arrived(s, p)
                attend(s * rows, rows)
                if d == 0:
                    keep.start()
                    continue
                for p in range(pieces):
                    give(d, p).start()
                continue
            for p in range(pieces):
                q_arrived(s, p)
                attend(s * rows + p * TILE, TILE)
                give(d, p).start()
    else:
        for s in range(n):
            q_arrived(s, 0)

        def step(g, carry):
            attend(g * group * TILE, group * TILE)
            return carry

        lax.fori_loop(0, tiles // group, step, 0)
        for d in range(1, n):
            give(d, 0).start()
        keep.start()

    for kind in (K, V):
        for d in order:
            if not (staged and d == 2):
                send(kind, d).wait_send()
    for d in order:
        for p in range(pieces):
            if not (staged and d == 2):
                q_send(d, p).wait_send()
    for kind in (K, V):
        for s in range(n):
            for side, sends, _, to, low, there, size in halo_copies(s):
                @pl.when(sends)
                def _():
                    halo(kind, s, side, to, low, there, size).wait_send()
    keep.wait()
    for d in range(1, n):
        s = partner(me, d, n)
        for p in range(pieces):
            there = out_ref.at[pl.ds(p * part, part), columns(s)]
            give(d, p).wait_send()
            pltpu.make_async_copy(there, there, o_recv.at[s, p]).wait()


def on_device(n, ctx_count, queries, keys, values, tile_lists, live_counts):
    tiles = tile_lists.shape[0]
    total = tiles * TILE
    window = total + 2 * HALO
    group = 3 if tiles % 3 == 0 else 1
    dma = pltpu.SemaphoreType.DMA
    return pl.pallas_call(
        functools.partial(kernel, n, ctx_count, tiles, group),
        out_shape=jax.ShapeDtypeStruct(queries.shape, jnp.bfloat16),
        in_specs=[
            pl.BlockSpec(memory_space=pltpu.HBM),
            pl.BlockSpec(memory_space=pltpu.HBM),
            pl.BlockSpec(memory_space=pltpu.HBM),
            pl.BlockSpec(memory_space=pltpu.HBM),
            pl.BlockSpec(memory_space=pltpu.HBM),
        ],
        out_specs=pl.BlockSpec(memory_space=pltpu.HBM),
        scratch_shapes=[
            pltpu.SMEM(live_counts.shape, jnp.int32),
            pltpu.VMEM(tile_lists.shape, jnp.int32),
            pltpu.VMEM((total, 2 * HDIM), jnp.bfloat16),
            pltpu.VMEM((window, 2 * HDIM), jnp.bfloat16),
            pltpu.VMEM((window, 2 * HDIM), jnp.bfloat16),
            pltpu.VMEM((total, HDIM), jnp.bfloat16),
            pltpu.VMEM((tiles, HDIM), jnp.float32),
            dma((2, n)),
            dma((2, n)),
            dma((n, group)),
            dma((n, group)),
            dma((2, 2, n)),
            dma((2, 2, n)),
            dma((n, group)),
            dma((n, group)),
            dma((3,)),
        ],
        compiler_params=pltpu.CompilerParams(
            collective_id=0, has_side_effects=True, vmem_limit_bytes=63 << 20
        ),
    )(live_counts, tile_lists, queries, keys, values)


def solution(mesh):
    return jax.shard_map(
        functools.partial(on_device, mesh.shape["head"], mesh.shape["ctx"]),
        mesh=mesh,
        in_specs=(
            P(("groups", "ctx", "head"), None),
            P(("groups", "ctx", "head"), None),
            P(("groups", "ctx", "head"), None),
            P(("groups", "ctx"), None),
            P(("groups", "ctx")),
        ),
        out_specs=P(("groups", "ctx", "head"), None),
        check_vma=False,
    )
```
